32 devices in a mesh: dp: 4 (over y, x), shard: 8 (over z, core).
Axes of the slice: x: 2, y: 2, z: 4, core: 2. Of those that a mesh axis runs over, the one named last changes fastest.
Arguments:
- stats_partial: float32 [4, 8, 2, 512, 512], P('dp', None, None, 'shard'), may hold values from -800 to 800, as said below
- gradient: bfloat16 [8, 512, 512], P(None, 'shard'), may hold values from -240 to 240
- owner_of: int32 [8], replicated, may hold values from 0 to 7, as said below
- layer_count: int32 [4], replicated, may hold values from 1 to 4, 8 in all
Outputs:
- preconditioned: bfloat16 [8, 2, 512, 512], P('shard', None, 'dp')
The draws below stay inside these ranges and needn't reach their ends.
Inputs may be any that keep to these rules, and one draw needn't show every extreme that they name: `owner_of`: each owner holds 0 to 2 blocks, and in every draw some owner holds exactly 2. `layer_count`: the counts sum to 8. `stats_partial`: each [512, 512] slice is symmetric positive definite.
All inputs are finite; a program needn't handle non-finite values.
Results may differ from the reference program's by a relative error of at most 0.0062.
The reference program's roundings to bfloat16 on the way (of `middle`) count: a program that leaves them out, or rounds other values in their place, can miss the bound.
Values may be sent and summed in bfloat16 or wider, within the bound.
A program may use at most 64 MiB of HBM per device.

```python
import math
import jax
import jax.numpy as jnp
import numpy as np
from jax import lax

B = 512
ITERS = 3
OCAP = 2
LAYERS = 4
NG = 8
N_DP = 4
N_SHARD = 8


def shared_signs(key):
    flips = jax.random.bernoulli(jax.random.fold_in(key, 91), 0.5, (NG, 2, B))
    return jnp.where(flips, 1.0, -1.0).astype(jnp.float32)


def draw_stats_partial(key, part):
    key_noise = jax.random.fold_in(jax.random.fold_in(key, 11), 0)
    key_rows = jax.random.fold_in(jax.random.fold_in(key, 11), 2)
    key_blocks = jax.random.fold_in(jax.random.fold_in(key, 11), 3)
    key_weight = jax.random.fold_in(jax.random.fold_in(key, 11), 4)
    full_shape = (N_DP, NG, 2, B, B)
    noise_all = jnp.clip(jax.random.normal(key_noise, full_shape, jnp.float32), -6.0, 6.0)
    row_top = 0.5 * jnp.log(10.0)
    symmetric = (noise_all + jnp.swapaxes(noise_all, -1, -2)) * (0.35 / jnp.sqrt(2.0 * B))
    direction = shared_signs(key) / jnp.sqrt(1.0 * B)
    weight_dense = jax.random.uniform(key_weight, (N_DP, NG, 2, 1, 1), jnp.float32, 3.0, 8.0)
    dense_part = weight_dense * direction[None, :, :, :, None] * direction[None, :, :, None, :]
    base_matrix = symmetric + jnp.eye(B, dtype=jnp.float32) + dense_part
    row_scale = jnp.exp(jax.random.uniform(key_rows, (N_DP, NG, 2, B), jnp.float32, 0.0, row_top))
    block_scale = jnp.exp(jax.random.uniform(key_blocks, (1, NG, 2, 1, 1), jnp.float32, jnp.log(0.05), jnp.log(20.0)))
    return base_matrix * row_scale[..., :, None] * row_scale[..., None, :] * block_scale


def draw_gradient(key, part):
    key_noise = jax.random.fold_in(jax.random.fold_in(key, 23), 0)
    key_rows = jax.random.fold_in(jax.random.fold_in(key, 23), 2)
    key_cols = jax.random.fold_in(jax.random.fold_in(key, 23), 3)
    key_blocks = jax.random.fold_in(jax.random.fold_in(key, 23), 4)
    key_left = jax.random.fold_in(jax.random.fold_in(key, 23), 5)
    key_right = jax.random.fold_in(jax.random.fold_in(key, 23), 6)
    full_shape = (NG, B, B)
    noise_all = jnp.clip(jax.random.normal(key_noise, full_shape, jnp.float32), -5.5, 5.5)
    signs = shared_signs(key)
    column_mix = jnp.clip(jax.random.normal(key_left, (NG, B), jnp.float32), -2.5, 2.5)
    row_mix = jnp.clip(jax.random.normal(key_right, (NG, B), jnp.float32), -2.5, 2.5)
    aligned = signs[:, 0, :, None] * column_mix[:, None, :] + row_mix[:, :, None] * signs[:, 1, None, :]
    mixed = 0.7 * noise_all + 0.45 * aligned
    row_ramp = 1.0 + 2.0 * jnp.arange(B, dtype=jnp.float32) / (B - 1)
    row_scale = row_ramp[None, :] * jnp.exp(jax.random.uniform(key_rows, (NG, B), jnp.float32, jnp.log(0.7), jnp.log(1.4)))
    col_scale = jnp.exp(jax.random.uniform(key_cols, (NG, B), jnp.float32, 0.0, jnp.log(3.0)))
    block_scale = jnp.exp(jax.random.uniform(key_blocks, (NG, 1, 1), jnp.float32, -jnp.log(3.0), jnp.log(3.0)))
    return (mixed * row_scale[:, :, None] * col_scale[:, None, :] * block_scale).astype(jnp.bfloat16)


def draw_owner_of(key, part):
    key_heavy, key_rank, key_order = jax.random.split(jax.random.fold_in(key, 37), 3)
    slot_count = N_SHARD * OCAP
    heavy_owner = jax.random.randint(key_heavy, (), 0, N_SHARD)
    ranks = jax.random.permutation(key_rank, slot_count).astype(jnp.int32)
    places = jnp.arange(slot_count, dtype=jnp.int32)
    scores = jnp.where(places // OCAP == heavy_owner, places - slot_count, ranks)
    forced = (places == 0) | (places == (N_SHARD - 1) * OCAP)
    scores = jnp.where(forced, jnp.minimum(scores, -1), scores).astype(jnp.int32)
    ordered = jnp.argsort(scores, stable=True)
    owners = (ordered[:NG] // OCAP).astype(jnp.int32)
    return jnp.take(owners, jax.random.permutation(key_order, NG)).astype(jnp.int32)


def profile(count, total, reach, lean):
    loads = [(1 << 20) // math.isqrt(grade ** lean) + 1 for grade in range(2, count + 1)]
    surplus, counts = total - reach - (count - 1), [1] * (count - 1)
    while surplus > 0:
        free = [i for i in range(count - 1) if counts[i] < reach]
        mass, remaining = sum([loads[i] for i in free]), surplus
        for i in free:
            more = min(reach - counts[i], max(1, remaining * loads[i] // mass), surplus)
            counts[i] = counts[i] + more
            surplus = surplus - more
    return np.array([reach] + counts)


def ragged_sizes(rng, number_of, total, limit, lean):
    if number_of == 2:
        one = jax.random.randint(rng, (), max(1, total - limit), min(limit, total - 1) + 1)
        return jnp.stack([one, total - one])
    sizes = jnp.asarray(profile(number_of, total, limit, lean), jnp.int32)
    couples = (number_of - 1) // 2
    donor, receiver = sizes[1:1 + 2 * couples:2], sizes[2:2 + 2 * couples:2]
    slack = jnp.minimum(donor - 1, limit - receiver)
    moved = jax.random.randint(jax.random.fold_in(rng, 1), (couples,), 0, 1 << 20) % (slack + 1)
    sizes = sizes.at[1:1 + 2 * couples:2].set(donor - moved).at[2:2 + 2 * couples:2].set(receiver + moved)
    return sizes[jax.random.permutation(jax.random.fold_in(rng, 2), number_of)]


def setup_inputs(seed: int = 0) -> dict:
    splits = jax.random.split(jax.random.key(seed), 5)
    return {
        "stats_partial": draw_stats_partial(jax.random.fold_in(splits[4], 71), 0),
        "gradient": draw_gradient(jax.random.fold_in(splits[4], 71), 0),
        "owner_of": draw_owner_of(jax.random.fold_in(splits[4], 71), 0),
        "layer_count": ragged_sizes(splits[3], LAYERS, NG, NG // 2, 2).astype(jnp.int32),
    }


highest = lax.Precision.HIGHEST

def product(left_side, right_side):
    return jnp.dot(left_side, right_side, precision=highest, preferred_element_type=jnp.float32)

def inverse_root(statistic):
    identity = jnp.eye(B, dtype=jnp.float32)
    magnitude = B * jnp.sqrt(jnp.mean(statistic * statistic) + 1e-06)
    matrix = statistic / magnitude
    factor = identity * magnitude ** (-0.25)
    for number in range(ITERS):
        update = (5.0 * identity - matrix) * 0.25
        factor = product(factor, update)
        if number + 1 < ITERS:
            square = product(update, update)
            fourth = product(square, square)
            matrix = product(fourth, matrix)
    return factor.astype(jnp.bfloat16)

def per_block(inputs):
    stat_pair, grad_block = inputs
    left_factor = inverse_root(stat_pair[0])
    right_factor = inverse_root(stat_pair[1])
    middle = jnp.dot(left_factor, grad_block, preferred_element_type=jnp.float32).astype(jnp.bfloat16)
    raw_block = jnp.dot(middle, right_factor, preferred_element_type=jnp.float32)
    grad_wide = grad_block.astype(jnp.float32)
    return (raw_block, jnp.sum(grad_wide * grad_wide), jnp.sum(raw_block * raw_block))

def reference(stats_partial, gradient, owner_of, layer_count):
    statistics = lax.optimization_barrier(jnp.sum(stats_partial, axis=0))
    raw_all, grad_sq, raw_sq = lax.map(per_block, (statistics, gradient))
    blocks = gradient.shape[0]
    block_ids = jnp.arange(blocks, dtype=jnp.int32)
    layer_ends = jnp.cumsum(layer_count).astype(jnp.int32)
    layer_of = lax.optimization_barrier(jnp.sum((block_ids[:, None] >= layer_ends[None, :]).astype(jnp.int32), axis=1))
    layer_hot = (layer_of[:, None] == jnp.arange(LAYERS, dtype=jnp.int32)[None, :]).astype(jnp.float32)
    grad_norms = lax.optimization_barrier(jnp.sum(layer_hot * grad_sq[:, None], axis=0))
    raw_norms = lax.optimization_barrier(jnp.sum(layer_hot * raw_sq[:, None], axis=0))
    graft_ratio = jnp.sqrt((grad_norms + 1e-06) / (raw_norms + 1e-06))
    block_scale = lax.optimization_barrier(jnp.sum(layer_hot * graft_ratio[None, :], axis=1))
    scaled = (raw_all * block_scale[:, None, None]).astype(jnp.bfloat16)
    same_owner = (owner_of[:, None] == owner_of[None, :]) & (block_ids[None, :] < block_ids[:, None])
    earlier = lax.optimization_barrier(jnp.sum(same_owner.astype(jnp.int32), axis=1)).astype(jnp.int32)
    output = jnp.zeros((N_SHARD, OCAP, B, B), jnp.bfloat16)
    return output.at[owner_of.astype(jnp.int32), earlier].set(scaled)
```

```python
import functools

import jax
import jax.numpy as jnp
from jax import lax
from jax.experimental import pallas as pl
from jax.experimental.pallas import tpu as pltpu
from jax.sharding import PartitionSpec as P

B = 512
ITERS = 3
OCAP = 2
LAYERS = 4


highest = lax.Precision.HIGHEST


def product(left_side, right_side):
    return jnp.dot(left_side, right_side, precision=highest, preferred_element_type=jnp.float32)


def inverse_root(statistic):
    identity = jnp.eye(B, dtype=jnp.float32)
    magnitude = B * jnp.sqrt(jnp.mean(statistic * statistic) + 1e-06)
    matrix = statistic / magnitude
    factor = identity * magnitude ** (-0.25)
    for number in range(ITERS):
        update = (5.0 * identity - matrix) * 0.25
        factor = product(factor, update)
        if number + 1 < ITERS:
            square = product(update, update)
            fourth = product(square, square)
            matrix = product(fourth, matrix)
    return factor.astype(jnp.bfloat16)


def precondition(left_all, right_all, grad_full, member, quarter):
    left_rows = lax.dynamic_slice_in_dim(left_all, member * quarter, quarter, 1)
    middle = jnp.einsum(
        "kqb,kbc->kqc", left_rows, grad_full, preferred_element_type=jnp.float32
    ).astype(jnp.bfloat16)
    result = jnp.einsum("kqc,kcd->kqd", middle, right_all, preferred_element_type=jnp.float32)
    grad_rows = lax.dynamic_slice_in_dim(grad_full, member * quarter, quarter, 1).astype(
        jnp.float32
    )
    return (
        result,
        jnp.sum(grad_rows * grad_rows, axis=(1, 2)),
        jnp.sum(result * result, axis=(1, 2)),
    )


def pick(array, index):
    flat = lax.map(
        lambda i: lax.dynamic_index_in_dim(array, i, 0, keepdims=False), index.reshape(-1)
    )
    return flat.reshape(index.shape + array.shape[1:])


def on_device(stats_partial, gradient, owner_of, layer_count):
    shards = lax.axis_size("shard")
    groups = lax.axis_size("dp")
    my_shard = lax.axis_index("shard")
    member = lax.axis_index("dp")
    blocks = owner_of.shape[0]
    quarter = B // groups
    block_ids = jnp.arange(blocks, dtype=jnp.int32)
    same_owner = (owner_of[:, None] == owner_of[None, :]) & (
        block_ids[None, :] < block_ids[:, None]
    )
    earlier = jnp.sum(same_owner.astype(jnp.int32), axis=1)
    target = owner_of * OCAP + earlier
    places = jnp.arange(shards * OCAP, dtype=jnp.int32)
    matches = target[:, None] == places[None, :]
    filled = jnp.any(matches, axis=0)
    chosen = jnp.sum(jnp.where(matches, block_ids[:, None], 0), axis=0)
    all_places = (
        jnp.arange(OCAP, dtype=jnp.int32)[:, None]
        + OCAP * jnp.arange(shards, dtype=jnp.int32)[None, :]
    )
    grad_pick = jnp.take(chosen, all_places)
    grad_live = jnp.take(filled, all_places)
    layer_ids = jnp.arange(LAYERS)
    layer_ends = jnp.sum(
        jnp.where(layer_ids[:, None] <= layer_ids[None, :], layer_count[:, None], 0), axis=0
    )
    layer_of = jnp.sum((block_ids[:, None] >= layer_ends[None, :]).astype(jnp.int32), axis=1)
    local = stats_partial[0]
    local_rows = local.shape[2]
    slot_index = member // 2
    members = jnp.arange(groups, dtype=jnp.int32)
    place_all = jnp.arange(shards, dtype=jnp.int32)[None, :] * OCAP + (members // 2)[:, None]
    pick_all = jnp.take(chosen, place_all)
    live_all = jnp.take(filled, place_all)
    flat_local = local.reshape(blocks * 2, local_rows, B)
    laid = jnp.where(
        live_all[:, :, None, None],
        pick(flat_local, pick_all * 2 + (members % 2)[:, None]),
        0.0,
    )
    outgoing = lax.psum_scatter(laid, "dp", scatter_dimension=0, tiled=True)[0]
    incoming = lax.all_to_all(outgoing, "shard", split_axis=0, concat_axis=0, tiled=True)
    statistic = incoming.reshape(B, B)
    my_blocks = jnp.take(chosen, my_shard * OCAP + jnp.arange(OCAP, dtype=jnp.int32))
    mine_live = jnp.take(filled, my_shard * OCAP + slot_index)
    statistic = jnp.where(mine_live, statistic, jnp.eye(B, dtype=jnp.float32))
    factor = inverse_root(statistic)
    factors = lax.all_gather(factor[None], "dp", axis=0, tiled=True).reshape(OCAP, 2, B, B)
    grad_send = jnp.where(
        grad_live[:, :, None, None],
        pick(gradient, grad_pick),
        jnp.zeros((), jnp.bfloat16),
    )
    grad_full = lax.all_to_all(grad_send, "shard", split_axis=1, concat_axis=1, tiled=True).reshape(
        OCAP, B, B
    )
    result, grad_terms, result_terms = precondition(
        factors[:, 0], factors[:, 1], grad_full, member, quarter
    )
    layer_hot = (
        jnp.take(layer_of, my_blocks)[:, None] == jnp.arange(LAYERS, dtype=jnp.int32)[None, :]
    ).astype(jnp.float32)
    grad_total, result_total = lax.psum(
        (
            jnp.sum(layer_hot * grad_terms[:, None], axis=0),
            jnp.sum(layer_hot * result_terms[:, None], axis=0),
        ),
        ("dp", "shard"),
    )
    graft_ratio = jnp.sqrt((grad_total + 1e-06) / (result_total + 1e-06))
    scaled = (result * jnp.sum(layer_hot * graft_ratio[None, :], axis=1)[:, None, None]).astype(
        jnp.bfloat16
    )
    return scaled[None]


MESH = pl.DeviceIdType.MESH


def root_of(total):
    n = total.shape[0]

    def times(a, b):
        return jnp.dot(
            a.astype(jnp.bfloat16), b.astype(jnp.bfloat16), preferred_element_type=jnp.float32
        )

    mean_square = jnp.sum(total * total, axis=(0, 1), keepdims=True) * (1.0 / (n * n))
    magnitude = n * jnp.sqrt(mean_square + 1e-06)
    scale = 1.0 / jnp.sqrt(jnp.sqrt(magnitude))

    def next_matrix(quarter):
        w = 2.5 * quarter - times(quarter, quarter)
        v = 3.125 * w - times(w, w)
        return 2.44140625 * quarter - times(v, quarter)

    first = total * (0.25 / magnitude)
    second = next_matrix(first)
    both = 1.25 * (first + second) - times(first, second)
    third = next_matrix(second)
    rest = 1.25 * both + 1.5625 * third - times(both, third)
    rows = lax.broadcasted_iota(jnp.int32, (n, n), 0)
    columns = lax.broadcasted_iota(jnp.int32, (n, n), 1)
    return ((jnp.where(rows == columns, 1.953125, 0.0) - rest) * scale).astype(jnp.bfloat16)


def refresh(
    shards, stats, grad, owner, counts, out,
    xs, xr, ys, yr, keep, zs, whole, gcols, factor, mid, midr, raw, gath, vec, vecr, vecs, vecz,
    x_sem, y_sem, z_sem, g_sem, h_sem, m_sem, r_sem, a_sem, f_sem, n_sem, o_sem, l_sem,
):
    s = lax.axis_index("shard")
    m = lax.axis_index("dp")
    x, y = lax.rem(m, 2), m // 2
    blocks, _, rows, n = stats.shape
    half, quarter = n // 2, n // 4
    x_peer, y_peer = y * 2 + 1 - x, (1 - y) * 2 + x
    diagonal = (1 - y) * 2 + 1 - x

    barrier = pltpu.get_barrier_semaphore()
    for d in (x_peer, y_peer, diagonal):
        pl.semaphore_signal(barrier, inc=1, device_id=(d, s), device_id_type=MESH)
    for k in range(1, shards):
        pl.semaphore_signal(
            barrier, inc=1, device_id=(m, lax.rem(s + k, shards)), device_id_type=MESH
        )

    def remote(source, target, sems, i, device):
        return pltpu.make_async_remote_copy(
            src_ref=source, dst_ref=target, send_sem=sems.at[0, i], recv_sem=sems.at[1, i],
            device_id=device, device_id_type=MESH,
        )

    def columns(which):
        return pl.ds(pl.multiple_of(which * half, half), half)

    def own_rows(which):
        return pl.ds(pl.multiple_of(which * rows, rows), rows)

    order = [lax.rem(s + k, shards) for k in range(shards)]
    for k in range(blocks):
        xs[k] = stats[order[k], 1 - x].astype(jnp.bfloat16)
    pl.semaphore_wait(barrier, shards + 2)

    x_copies, y_copies, z_copies, g_copies = [], [], [], []
    for k in range(blocks):
        c = remote(xs.at[k], xr.at[k], x_sem, k, (x_peer, s))
        c.start()
        x_copies.append(c)
    for k in range(1, shards):
        c = remote(
            grad.at[order[k], :, columns(y)], gcols.at[own_rows(s)], g_sem, k, (m, order[k])
        )
        c.start()
        g_copies.append(c)
    local = pltpu.make_async_copy(
        grad.at[s, :, columns(y)], gcols.at[own_rows(s)], l_sem.at[0]
    )
    local.start()
    lanes = lax.broadcasted_iota(jnp.int32, (8, 128), 1)
    lane_row = lax.broadcasted_iota(jnp.int32, (8, 128), 0)
    squares = jnp.zeros((8, 128), jnp.float32)
    for b in range(blocks):
        g = grad[b].astype(jnp.float32)
        squares = jnp.where(
            (lane_row == 1) & (lanes == b),
            jnp.sum(g * g, axis=(0, 1), keepdims=True) * 0.25,
            squares,
        )
    for t in range(blocks + 2):
        if t < blocks:
            x_copies[t].wait_recv()
            mine = stats[order[t], x] + xr[t].astype(jnp.float32)
            left, right = mine[:, :half], mine[:, half:]
            keep[t] = jnp.where(y == 0, left, right)
            ys[t] = jnp.where(y == 0, right, left).astype(jnp.bfloat16)
            c = remote(ys.at[t], yr.at[t], y_sem, t, (y_peer, s))
            c.start()
            y_copies.append(c)
        if t >= 2:
            k = t - 2
            y_copies[k].wait_recv()
            zs[k] = (keep[k] + yr[k].astype(jnp.float32)).astype(jnp.bfloat16)
            if k > 0:
                c = remote(zs.at[k], whole.at[y, own_rows(s)], z_sem, k, (m, order[k]))
                c.start()
                z_copies.append(c)
    own = pltpu.make_async_copy(zs.at[0], whole.at[y, own_rows(s)], l_sem.at[1])
    own.start()
    own.wait()
    for c in z_copies:
        c.wait_recv()
    h_copy = remote(whole.at[y], whole.at[y], h_sem, 0, (y_peer, s))
    h_copy.start()
    h_copy.wait_recv()
    factor[...] = root_of(
        jnp.concatenate([whole[0], whole[1]], axis=1).astype(jnp.float32)
    )
    local.wait()
    for c in g_copies:
        c.wait_recv()

    piece = pl.ds(0, quarter)
    other = remote(raw.at[piece], gath.at[s], r_sem, 0, (x_peer, s))

    @pl.when(x == 0)
    def _():
        mid[...] = jnp.dot(
            factor[...], gcols[...], preferred_element_type=jnp.float32
        ).astype(jnp.bfloat16)
        a = remote(mid.at[columns(y)], midr.at[y], m_sem, 0, (x_peer, s))
        b = remote(mid.at[columns(1 - y)], midr.at[y], m_sem, 1, (diagonal, s))
        b.start()
        a.start()
        vec[...] = squares
        a.wait_send()
        b.wait_send()
        other.wait_recv()

    @pl.when(x == 1)
    def _():
        a = remote(mid.at[columns(y)], midr.at[y], m_sem, 0, (x_peer, s))
        b = remote(mid.at[columns(1 - y)], midr.at[1 - y], m_sem, 1, (diagonal, s))
        a.wait_recv()
        b.wait_recv()
        result = jnp.dot(midr[0], factor[:half], preferred_element_type=jnp.float32) + jnp.dot(
            midr[1], factor[half:], preferred_element_type=jnp.float32
        )
        raw[...] = result.astype(jnp.bfloat16)
        other.start()
        gath[s] = raw[quarter:]
        vec[...] = jnp.where(
            (lane_row == 0) & (lanes == s),
            jnp.sum(result * result, axis=(0, 1), keepdims=True),
            squares,
        )
        other.wait_send()

    neighbour = s + 1 - 2 * lax.rem(s, 2)
    far, near = [], []
    for k in range(1, shards // 2):
        c = remote(gath.at[s], gath.at[s], a_sem, k, (m, order[2 * k]))
        c.start()
        far.append(c)
    c = remote(gath.at[s], gath.at[s], f_sem, 0, (m, neighbour))
    c.start()
    near.append(c)
    norms = []
    for i, d in enumerate((x_peer, y_peer, diagonal)):
        c = remote(vec, vecr.at[i], n_sem, i, (d, s))
        c.start()
        norms.append(c)
    for c in norms:
        c.wait_recv()
    vecs[...] = vec[...] + vecr[0] + vecr[1] + vecr[2]
    for k in range(1, shards):
        c = remote(vecs, vecz.at[k - 1], o_sem, k, (m, order[k]))
        c.start()
        norms.append(c)

    for k in range(1, shards // 2):
        far[k - 1].wait_recv()
        origin = lax.rem(s + shards - 2 * k, shards)
        c = remote(gath.at[origin], gath.at[origin], f_sem, k, (m, neighbour))
        c.start()
        near.append(c)
    for c in norms[3:]:
        c.wait_recv()
    totals = vecs[...] + jnp.sum(vecz[...], axis=0)
    raw_sq, grad_sq = totals[0:1], totals[1:2]

    ends, layer = [], []
    for l in range(counts.shape[0]):
        ends.append(counts[l] + (ends[-1] if ends else 0))
    for b in range(blocks):
        layer.append(sum(jnp.where(b >= e, 1, 0) for e in ends))
    count = jnp.int32(0)
    chosen = [jnp.int32(0)] * OCAP
    chosen_layer = [jnp.int32(-1)] * OCAP
    for b in range(blocks):
        is_mine = owner[b] == s
        for k in range(OCAP):
            hit = is_mine & (count == k)
            chosen[k] = jnp.where(hit, b, chosen[k])
            chosen_layer[k] = jnp.where(hit, layer[b], chosen_layer[k])
        count = count + jnp.where(is_mine, 1, 0)
    lane = lax.broadcasted_iota(jnp.int32, (1, 128), 1)
    layer_lane = jnp.full((1, 128), -2, jnp.int32)
    for b in range(blocks):
        layer_lane = jnp.where(lane == b, layer[b], layer_lane)
    scales = []
    for k in range(OCAP):
        same = layer_lane == chosen_layer[k]
        top = jnp.sum(jnp.where(same, grad_sq, 0.0), axis=1, keepdims=True)
        bottom = jnp.sum(jnp.where(same, raw_sq, 0.0), axis=1, keepdims=True)
        live = jnp.where(count > k, 1.0, 0.0)
        scales.append(live * jnp.sqrt((top + 1e-06) / (bottom + 1e-06)))

    for c in near:
        c.wait_recv()
    for k in range(OCAP):
        out[k] = (gath[chosen[k]].astype(jnp.float32) * scales[k]).astype(jnp.bfloat16)
    for c in x_copies + y_copies + z_copies + g_copies + [h_copy] + far + near + norms:
        c.wait_send()


def refreshed(stats_partial, gradient, owner_of, layer_count):
    shards = lax.axis_size("shard")
    stats = stats_partial[0]
    blocks, _, rows, n = stats.shape
    half, quarter = n // 2, n // 4
    bf16, f32 = jnp.bfloat16, jnp.float32
    vmem = pltpu.VMEM
    sems = lambda count: pltpu.SemaphoreType.DMA((2, count))
    out = pl.pallas_call(
        functools.partial(refresh, shards),
        out_shape=jax.ShapeDtypeStruct((OCAP, quarter, n), bf16),
        in_specs=[pl.BlockSpec(memory_space=pltpu.VMEM)] * 2
        + [pl.BlockSpec(memory_space=pltpu.SMEM)] * 2,
        out_specs=pl.BlockSpec(memory_space=pltpu.VMEM),
        scratch_shapes=[
            vmem((blocks, rows, n), bf16),
            vmem((blocks, rows, n), bf16),
            vmem((blocks, rows, half), bf16),
            vmem((blocks, rows, half), bf16),
            vmem((blocks, rows, half), f32),
            vmem((blocks, rows, half), bf16),
            vmem((2, n, half), bf16),
            vmem((n, half), bf16),
            vmem((n, n), bf16),
            vmem((n, half), bf16),
            vmem((2, half, half), bf16),
            vmem((half, n), bf16),
            vmem((blocks, quarter, n), bf16),
            vmem((8, 128), f32),
            vmem((3, 8, 128), f32),
            vmem((8, 128), f32),
            vmem((shards - 1, 8, 128), f32),
            sems(blocks),
            sems(blocks),
            sems(blocks),
            sems(shards),
            sems(1),
            sems(2),
            sems(1),
            sems(shards // 2),
            sems(shards // 2),
            sems(3),
            sems(shards),
            pltpu.SemaphoreType.DMA((2,)),
        ],
        compiler_params=pltpu.CompilerParams(
            collective_id=0, has_side_effects=True, vmem_limit_bytes=48 * 2**20
        ),
    )(stats, gradient, owner_of, layer_count)
    return out[None]


def solution(mesh):
    placed = (P("dp", None, None, "shard", None), P(None, "shard", None), P(), P())
    groups, shards = mesh.shape["dp"], mesh.shape["shard"]

    def program(stats_partial, gradient, owner_of, layer_count):
        blocks, strip = owner_of.shape[0], stats_partial.shape[3]
        fits = (groups, blocks) == (4, shards) and shards % 2 == 0 and strip % 16 == 0
        body = refreshed if fits and blocks <= 128 else on_device
        return body(stats_partial, gradient, owner_of, layer_count)

    return jax.shard_map(
        program,
        mesh=mesh,
        in_specs=placed,
        out_specs=P("shard", None, "dp", None),
        check_vma=False,
    )
```

```python
import functools

import jax
import jax.numpy as jnp
from jax import lax
from jax.experimental import pallas as pl
from jax.experimental.pallas import tpu as pltpu
from jax.sharding import PartitionSpec as P

B = 512
ITERS = 3
OCAP = 2
LAYERS = 4


highest = lax.Precision.HIGHEST


def product(left_side, right_side):
    return jnp.dot(left_side, right_side, precision=highest, preferred_element_type=jnp.float32)


def inverse_root(statistic):
    identity = jnp.eye(B, dtype=jnp.float32)
    magnitude = B * jnp.sqrt(jnp.mean(statistic * statistic) + 1e-06)
    matrix = statistic / magnitude
    factor = identity * magnitude ** (-0.25)
    for number in range(ITERS):
        update = (5.0 * identity - matrix) * 0.25
        factor = product(factor, update)
        if number + 1 < ITERS:
            square = product(update, update)
            fourth = product(square, square)
            matrix = product(fourth, matrix)
    return factor.astype(jnp.bfloat16)


def precondition(left_all, right_all, grad_full, member, quarter):
    left_rows = lax.dynamic_slice_in_dim(left_all, member * quarter, quarter, 1)
    middle = jnp.einsum(
        "kqb,kbc->kqc", left_rows, grad_full, preferred_element_type=jnp.float32
    ).astype(jnp.bfloat16)
    result = jnp.einsum("kqc,kcd->kqd", middle, right_all, preferred_element_type=jnp.float32)
    grad_rows = lax.dynamic_slice_in_dim(grad_full, member * quarter, quarter, 1).astype(
        jnp.float32
    )
    return (
        result,
        jnp.sum(grad_rows * grad_rows, axis=(1, 2)),
        jnp.sum(result * result, axis=(1, 2)),
    )


def pick(array, index):
    flat = lax.map(
        lambda i: lax.dynamic_index_in_dim(array, i, 0, keepdims=False), index.reshape(-1)
    )
    return flat.reshape(index.shape + array.shape[1:])


def on_device(stats_partial, gradient, owner_of, layer_count):
    shards = lax.axis_size("shard")
    groups = lax.axis_size("dp")
    my_shard = lax.axis_index("shard")
    member = lax.axis_index("dp")
    blocks = owner_of.shape[0]
    quarter = B // groups
    block_ids = jnp.arange(blocks, dtype=jnp.int32)
    same_owner = (owner_of[:, None] == owner_of[None, :]) & (
        block_ids[None, :] < block_ids[:, None]
    )
    earlier = jnp.sum(same_owner.astype(jnp.int32), axis=1)
    target = owner_of * OCAP + earlier
    places = jnp.arange(shards * OCAP, dtype=jnp.int32)
    matches = target[:, None] == places[None, :]
    filled = jnp.any(matches, axis=0)
    chosen = jnp.sum(jnp.where(matches, block_ids[:, None], 0), axis=0)
    all_places = (
        jnp.arange(OCAP, dtype=jnp.int32)[:, None]
        + OCAP * jnp.arange(shards, dtype=jnp.int32)[None, :]
    )
    grad_pick = jnp.take(chosen, all_places)
    grad_live = jnp.take(filled, all_places)
    layer_ids = jnp.arange(LAYERS)
    layer_ends = jnp.sum(
        jnp.where(layer_ids[:, None] <= layer_ids[None, :], layer_count[:, None], 0), axis=0
    )
    layer_of = jnp.sum((block_ids[:, None] >= layer_ends[None, :]).astype(jnp.int32), axis=1)
    local = stats_partial[0]
    local_rows = local.shape[2]
    slot_index = member // 2
    members = jnp.arange(groups, dtype=jnp.int32)
    place_all = jnp.arange(shards, dtype=jnp.int32)[None, :] * OCAP + (members // 2)[:, None]
    pick_all = jnp.take(chosen, place_all)
    live_all = jnp.take(filled, place_all)
    flat_local = local.reshape(blocks * 2, local_rows, B)
    laid = jnp.where(
        live_all[:, :, None, None],
        pick(flat_local, pick_all * 2 + (members % 2)[:, None]),
        0.0,
    )
    outgoing = lax.psum_scatter(laid, "dp", scatter_dimension=0, tiled=True)[0]
    incoming = lax.all_to_all(outgoing, "shard", split_axis=0, concat_axis=0, tiled=True)
    statistic = incoming.reshape(B, B)
    my_blocks = jnp.take(chosen, my_shard * OCAP + jnp.arange(OCAP, dtype=jnp.int32))
    mine_live = jnp.take(filled, my_shard * OCAP + slot_index)
    statistic = jnp.where(mine_live, statistic, jnp.eye(B, dtype=jnp.float32))
    factor = inverse_root(statistic)
    factors = lax.all_gather(factor[None], "dp", axis=0, tiled=True).reshape(OCAP, 2, B, B)
    grad_send = jnp.where(
        grad_live[:, :, None, None],
        pick(gradient, grad_pick),
        jnp.zeros((), jnp.bfloat16),
    )
    grad_full = lax.all_to_all(grad_send, "shard", split_axis=1, concat_axis=1, tiled=True).reshape(
        OCAP, B, B
    )
    result, grad_terms, result_terms = precondition(
        factors[:, 0], factors[:, 1], grad_full, member, quarter
    )
    layer_hot = (
        jnp.take(layer_of, my_blocks)[:, None] == jnp.arange(LAYERS, dtype=jnp.int32)[None, :]
    ).astype(jnp.float32)
    grad_total, result_total = lax.psum(
        (
            jnp.sum(layer_hot * grad_terms[:, None], axis=0),
            jnp.sum(layer_hot * result_terms[:, None], axis=0),
        ),
        ("dp", "shard"),
    )
    graft_ratio = jnp.sqrt((grad_total + 1e-06) / (result_total + 1e-06))
    scaled = (result * jnp.sum(layer_hot * graft_ratio[None, :], axis=1)[:, None, None]).astype(
        jnp.bfloat16
    )
    return scaled[None]


MESH = pl.DeviceIdType.MESH
PIECES = 2


def root_of(total):
    n = total.shape[0]

    def times(a, b):
        return jnp.dot(
            a.astype(jnp.bfloat16), b.astype(jnp.bfloat16), preferred_element_type=jnp.float32
        )

    mean_square = jnp.sum(total * total, axis=(0, 1), keepdims=True) * (1.0 / (n * n))
    magnitude = n * jnp.sqrt(mean_square + 1e-06)
    scale = 1.0 / jnp.sqrt(jnp.sqrt(magnitude))

    def next_matrix(quarter):
        w = 2.5 * quarter - times(quarter, quarter)
        v = 3.125 * w - times(w, w)
        return 2.44140625 * quarter - times(v, quarter)

    first = total * (0.25 / magnitude)
    second = next_matrix(first)
    both = 1.25 * (first + second) - times(first, second)
    third = next_matrix(second)
    rest = 1.25 * both + 1.5625 * third - times(both, third)
    rows = lax.broadcasted_iota(jnp.int32, (n, n), 0)
    columns = lax.broadcasted_iota(jnp.int32, (n, n), 1)
    return ((jnp.where(rows == columns, 1.953125, 0.0) - rest) * scale).astype(jnp.bfloat16)


def refresh(
    shards, stats_in, grad_in, owner_in, counts_in, out, theirs, ours, grad, owner, counts,
    xs, xr, ys, yr, keep, zs, whole, gcols, factor, mid, midr, raw, gath, vec, vecr, vecs, vecz,
    x_sem, y_sem, z_sem, g_sem, h_sem, m_sem, r_sem, a_sem, f_sem, n_sem, o_sem, l_sem,
):
    s = lax.axis_index("shard")
    m = lax.axis_index("dp")
    x, y = lax.rem(m, 2), m // 2
    blocks, rows, n = theirs.shape
    half, quarter = n // 2, n // 4
    piece = quarter // PIECES
    x_peer, y_peer = y * 2 + 1 - x, (1 - y) * 2 + x
    diagonal = (1 - y) * 2 + 1 - x

    loads = [
        pltpu.make_async_copy(source, target, l_sem.at[i])
        for i, (source, target) in enumerate(
            (
                (stats_in.at[:, 1 - x], theirs),
                (stats_in.at[:, x], ours),
                (grad_in, grad),
                (owner_in, owner),
                (counts_in, counts),
            )
        )
    ]
    for c in loads:
        c.start()
    barrier = pltpu.get_barrier_semaphore()
    for d in (x_peer, y_peer, diagonal):
        pl.semaphore_signal(barrier, inc=1, device_id=(d, s), device_id_type=MESH)
    for k in range(1, shards):
        pl.semaphore_signal(
            barrier, inc=1, device_id=(m, lax.rem(s + k, shards)), device_id_type=MESH
        )

    def remote(source, target, sems, i, device):
        return pltpu.make_async_remote_copy(
            src_ref=source, dst_ref=target, send_sem=sems.at[0, i], recv_sem=sems.at[1, i],
            device_id=device, device_id_type=MESH,
        )

    def columns(which):
        return pl.ds(pl.multiple_of(which * half, half), half)

    def own_rows(which):
        return pl.ds(pl.multiple_of(which * rows, rows), rows)

    order = [lax.rem(s + k, shards) for k in range(shards)]
    loads[0].wait()
    for k in range(blocks):
        xs[k] = theirs[order[k]].astype(jnp.bfloat16)
    pl.semaphore_wait(barrier, shards + 2)

    x_copies, y_copies, z_copies, g_copies = [], [], [], []
    for k in range(blocks):
        c = remote(xs.at[k], xr.at[k], x_sem, k, (x_peer, s))
        c.start()
        x_copies.append(c)
    loads[1].wait()
    loads[2].wait()
    for k in range(1, shards):
        c = remote(
            grad.at[order[k], :, columns(y)], gcols.at[own_rows(s)], g_sem, k, (m, order[k])
        )
        c.start()
        g_copies.append(c)
    local = pltpu.make_async_copy(
        grad.at[s, :, columns(y)], gcols.at[own_rows(s)], l_sem.at[5]
    )
    local.start()
    lanes = lax.broadcasted_iota(jnp.int32, (8, 128), 1)
    lane_row = lax.broadcasted_iota(jnp.int32, (8, 128), 0)
    squares = jnp.zeros((8, 128), jnp.float32)
    for b in range(blocks):
        g = grad[b].astype(jnp.float32)
        squares = jnp.where(
            (lane_row == 1) & (lanes == b),
            jnp.sum(g * g, axis=(0, 1), keepdims=True) * 0.25,
            squares,
        )
    for t in range(blocks + 2):
        if t < blocks:
            x_copies[t].wait_recv()
            mine = ours[order[t]] + xr[t].astype(jnp.float32)
            left, right = mine[:, :half], mine[:, half:]
            keep[t] = jnp.where(y == 0, left, right)
            ys[t] = jnp.where(y == 0, right, left).astype(jnp.bfloat16)
            c = remote(ys.at[t], yr.at[t], y_sem, t, (y_peer, s))
            c.start()
            y_copies.append(c)
        if t >= 2:
            k = t - 2
            y_copies[k].wait_recv()
            zs[k] = (keep[k] + yr[k].astype(jnp.float32)).astype(jnp.bfloat16)
            if k > 0:
                c = remote(zs.at[k], whole.at[y, own_rows(s)], z_sem, k, (m, order[k]))
                c.start()
                z_copies.append(c)
    own = pltpu.make_async_copy(zs.at[0], whole.at[y, own_rows(s)], l_sem.at[6])
    own.start()
    own.wait()
    h_copies = []
    for k in range(blocks):
        if k > 0:
            z_copies[k - 1].wait_recv()
        at = whole.at[y, own_rows(lax.rem(s + shards - k, shards))]
        c = remote(at, at, h_sem, k, (y_peer, s))
        c.start()
        h_copies.append(c)
    for c in h_copies:
        c.wait_recv()
    factor[...] = root_of(
        jnp.concatenate([whole[0], whole[1]], axis=1).astype(jnp.float32)
    )
    local.wait()
    for c in g_copies:
        c.wait_recv()

    levels = shards // 2
    neighbour = s + 1 - 2 * lax.rem(s, 2)

    def part(i):
        return pl.ds(i * piece, piece)

    def across(i):
        return remote(raw.at[part(i)], gath.at[s, part(i)], r_sem, i, (x_peer, s))

    def along(k, i):
        at = gath.at[s, part(i)]
        return remote(at, at, a_sem, k * PIECES + i, (m, order[2 * k]))

    def sideways(k, i):
        at = gath.at[lax.rem(s + shards - 2 * k, shards), part(i)]
        return remote(at, at, f_sem, k * PIECES + i, (m, neighbour))

    def spread(i):
        for k in range(1, levels):
            along(k, i).start()
        sideways(0, i).start()

    turns = [i + q * PIECES for q in (0, 1) for i in range(PIECES)]

    @pl.when(x == 0)
    def _():
        sent = []
        for t in turns:
            for slot, (to, d) in enumerate(((1 - y, diagonal), (y, x_peer))):
                at = pl.ds(pl.multiple_of(to * half + t * piece, piece), piece)
                mid[at] = jnp.dot(
                    factor[at], gcols[...], preferred_element_type=jnp.float32
                ).astype(jnp.bfloat16)
                c = remote(mid.at[at], midr.at[y, part(t)], m_sem, 2 * t + slot, (d, s))
                c.start()
                sent.append(c)
        vec[...] = squares
        for i in range(PIECES):
            across(i).wait_recv()
            spread(i)
        for c in sent:
            c.wait_send()

    @pl.when(x == 1)
    def _():
        total = jnp.zeros((1, 1), jnp.float32)
        for t in turns:
            for slot, (source, d) in enumerate(((1 - y, diagonal), (y, x_peer))):
                at = midr.at[source, part(t)]
                remote(at, at, m_sem, 2 * t + slot, (d, s)).wait_recv()
            result = jnp.dot(
                midr[0, part(t)], factor[:half], preferred_element_type=jnp.float32
            ) + jnp.dot(midr[1, part(t)], factor[half:], preferred_element_type=jnp.float32)
            if t < PIECES:
                raw[part(t)] = result.astype(jnp.bfloat16)
                across(t).start()
            else:
                gath[s, part(t - PIECES)] = result.astype(jnp.bfloat16)
                spread(t - PIECES)
            total = total + jnp.sum(result * result, axis=(0, 1), keepdims=True)
        vec[...] = jnp.where((lane_row == 0) & (lanes == s), total, squares)
        for i in range(PIECES):
            across(i).wait_send()

    norms = []
    for i, d in enumerate((x_peer, y_peer, diagonal)):
        c = remote(vec, vecr.at[i], n_sem, i, (d, s))
        c.start()
        norms.append(c)

    for c in norms:
        c.wait_recv()
    vecs[...] = vec[...] + vecr[0] + vecr[1] + vecr[2]
    for k in range(1, shards):
        c = remote(vecs, vecz.at[k - 1], o_sem, k, (m, order[k]))
        c.start()
        norms.append(c)
    for i in range(PIECES):
        for k in range(1, levels):
            along(k, i).wait_recv()
            sideways(k, i).start()
    for c in norms[3:]:
        c.wait_recv()
    loads[3].wait()
    loads[4].wait()
    totals = vecs[...] + jnp.sum(vecz[...], axis=0)
    raw_sq, grad_sq = totals[0:1], totals[1:2]

    ends, layer = [], []
    for l in range(counts.shape[0]):
        ends.append(counts[l] + (ends[-1] if ends else 0))
    for b in range(blocks):
        layer.append(sum(jnp.where(b >= e, 1, 0) for e in ends))
    count = jnp.int32(0)
    chosen = [jnp.int32(0)] * OCAP
    chosen_layer = [jnp.int32(-1)] * OCAP
    for b in range(blocks):
        is_mine = owner[b] == s
        for k in range(OCAP):
            hit = is_mine & (count == k)
            chosen[k] = jnp.where(hit, b, chosen[k])
            chosen_layer[k] = jnp.where(hit, layer[b], chosen_layer[k])
        count = count + jnp.where(is_mine, 1, 0)
    lane = lax.broadcasted_iota(jnp.int32, (1, 128), 1)
    layer_lane = jnp.full((1, 128), -2, jnp.int32)
    for b in range(blocks):
        layer_lane = jnp.where(lane == b, layer[b], layer_lane)
    scales = []
    for k in range(OCAP):
        same = layer_lane == chosen_layer[k]
        top = jnp.sum(jnp.where(same, grad_sq, 0.0), axis=1, keepdims=True)
        bottom = jnp.sum(jnp.where(same, raw_sq, 0.0), axis=1, keepdims=True)
        live = jnp.where(count > k, 1.0, 0.0)
        scales.append(live * jnp.sqrt((top + 1e-06) / (bottom + 1e-06)))

    for i in range(PIECES):
        for k in range(levels):
            sideways(k, i).wait_recv()
    for k in range(OCAP):
        out[k] = (gath[chosen[k]].astype(jnp.float32) * scales[k]).astype(jnp.bfloat16)
    for c in x_copies + y_copies + z_copies + g_copies + h_copies + norms:
        c.wait_send()
    for i in range(PIECES):
        for k in range(levels):
            sideways(k, i).wait_send()
            if k:
                along(k, i).wait_send()


def refreshed(stats_partial, gradient, owner_of, layer_count):
    shards = lax.axis_size("shard")
    stats = stats_partial[0]
    blocks, _, rows, n = stats.shape
    half, quarter = n // 2, n // 4
    bf16, f32 = jnp.bfloat16, jnp.float32
    vmem = pltpu.VMEM
    sems = lambda count: pltpu.SemaphoreType.DMA((2, count))
    out = pl.pallas_call(
        functools.partial(refresh, shards),
        out_shape=jax.ShapeDtypeStruct((OCAP, quarter, n), bf16),
        in_specs=[pl.BlockSpec(memory_space=pltpu.HBM)] * 4,
        out_specs=pl.BlockSpec(memory_space=pltpu.VMEM),
        scratch_shapes=[
            vmem((blocks, rows, n), f32),
            vmem((blocks, rows, n), f32),
            vmem((blocks, rows, n), bf16),
            pltpu.SMEM(owner_of.shape, jnp.int32),
            pltpu.SMEM(layer_count.shape, jnp.int32),
            vmem((blocks, rows, n), bf16),
            vmem((blocks, rows, n), bf16),
            vmem((blocks, rows, half), bf16),
            vmem((blocks, rows, half), bf16),
            vmem((blocks, rows, half), f32),
            vmem((blocks, rows, half), bf16),
            vmem((2, n, half), bf16),
            vmem((n, half), bf16),
            vmem((n, n), bf16),
            vmem((n, half), bf16),
            vmem((2, half, half), bf16),
            vmem((quarter, n), bf16),
            vmem((blocks, quarter, n), bf16),
            vmem((8, 128), f32),
            vmem((3, 8, 128), f32),
            vmem((8, 128), f32),
            vmem((shards - 1, 8, 128), f32),
            sems(blocks),
            sems(blocks),
            sems(blocks),
            sems(shards),
            sems(blocks),
            sems(4 * PIECES),
            sems(PIECES),
            sems(shards // 2 * PIECES),
            sems(shards // 2 * PIECES),
            sems(3),
            sems(shards),
            pltpu.SemaphoreType.DMA((7,)),
        ],
        compiler_params=pltpu.CompilerParams(
            collective_id=0, has_side_effects=True, vmem_limit_bytes=62 * 2**20
        ),
    )(stats, gradient, owner_of, layer_count)
    return out[None]


def solution(mesh):
    placed = (P("dp", None, None, "shard", None), P(None, "shard", None), P(), P())
    groups, shards = mesh.shape["dp"], mesh.shape["shard"]

    def program(stats_partial, gradient, owner_of, layer_count):
        blocks, strip = owner_of.shape[0], stats_partial.shape[3]
        fits = (groups, blocks) == (4, shards) and shards % 2 == 0 and strip % 16 == 0
        body = refreshed if fits and blocks <= 128 else on_device
        return body(stats_partial, gradient, owner_of, layer_count)

    return jax.shard_map(
        program,
        mesh=mesh,
        in_specs=placed,
        out_specs=P("shard", None, "dp", None),
        check_vma=False,
    )
```

```python
import functools

import jax
import jax.numpy as jnp
from jax import lax
from jax.experimental import pallas as pl
from jax.experimental.pallas import tpu as pltpu
from jax.sharding import PartitionSpec as P

B = 512
ITERS = 3
OCAP = 2
LAYERS = 4


highest = lax.Precision.HIGHEST


def product(left_side, right_side):
    return jnp.dot(left_side, right_side, precision=highest, preferred_element_type=jnp.float32)


def inverse_root(statistic):
    identity = jnp.eye(B, dtype=jnp.float32)
    magnitude = B * jnp.sqrt(jnp.mean(statistic * statistic) + 1e-06)
    matrix = statistic / magnitude
    factor = identity * magnitude ** (-0.25)
    for number in range(ITERS):
        update = (5.0 * identity - matrix) * 0.25
        factor = product(factor, update)
        if number + 1 < ITERS:
            square = product(update, update)
            fourth = product(square, square)
            matrix = product(fourth, matrix)
    return factor.astype(jnp.bfloat16)


def precondition(left_all, right_all, grad_full, member, quarter):
    left_rows = lax.dynamic_slice_in_dim(left_all, member * quarter, quarter, 1)
    middle = jnp.einsum(
        "kqb,kbc->kqc", left_rows, grad_full, preferred_element_type=jnp.float32
    ).astype(jnp.bfloat16)
    result = jnp.einsum("kqc,kcd->kqd", middle, right_all, preferred_element_type=jnp.float32)
    grad_rows = lax.dynamic_slice_in_dim(grad_full, member * quarter, quarter, 1).astype(
        jnp.float32
    )
    return (
        result,
        jnp.sum(grad_rows * grad_rows, axis=(1, 2)),
        jnp.sum(result * result, axis=(1, 2)),
    )


def pick(array, index):
    flat = lax.map(
        lambda i: lax.dynamic_index_in_dim(array, i, 0, keepdims=False), index.reshape(-1)
    )
    return flat.reshape(index.shape + array.shape[1:])


def on_device(stats_partial, gradient, owner_of, layer_count):
    shards = lax.axis_size("shard")
    groups = lax.axis_size("dp")
    my_shard = lax.axis_index("shard")
    member = lax.axis_index("dp")
    blocks = owner_of.shape[0]
    quarter = B // groups
    block_ids = jnp.arange(blocks, dtype=jnp.int32)
    same_owner = (owner_of[:, None] == owner_of[None, :]) & (
        block_ids[None, :] < block_ids[:, None]
    )
    earlier = jnp.sum(same_owner.astype(jnp.int32), axis=1)
    target = owner_of * OCAP + earlier
    places = jnp.arange(shards * OCAP, dtype=jnp.int32)
    matches = target[:, None] == places[None, :]
    filled = jnp.any(matches, axis=0)
    chosen = jnp.sum(jnp.where(matches, block_ids[:, None], 0), axis=0)
    all_places = (
        jnp.arange(OCAP, dtype=jnp.int32)[:, None]
        + OCAP * jnp.arange(shards, dtype=jnp.int32)[None, :]
    )
    grad_pick = jnp.take(chosen, all_places)
    grad_live = jnp.take(filled, all_places)
    layer_ids = jnp.arange(LAYERS)
    layer_ends = jnp.sum(
        jnp.where(layer_ids[:, None] <= layer_ids[None, :], layer_count[:, None], 0), axis=0
    )
    layer_of = jnp.sum((block_ids[:, None] >= layer_ends[None, :]).astype(jnp.int32), axis=1)
    local = stats_partial[0]
    local_rows = local.shape[2]
    slot_index = member // 2
    members = jnp.arange(groups, dtype=jnp.int32)
    place_all = jnp.arange(shards, dtype=jnp.int32)[None, :] * OCAP + (members // 2)[:, None]
    pick_all = jnp.take(chosen, place_all)
    live_all = jnp.take(filled, place_all)
    flat_local = local.reshape(blocks * 2, local_rows, B)
    laid = jnp.where(
        live_all[:, :, None, None],
        pick(flat_local, pick_all * 2 + (members % 2)[:, None]),
        0.0,
    )
    outgoing = lax.psum_scatter(laid, "dp", scatter_dimension=0, tiled=True)[0]
    incoming = lax.all_to_all(outgoing, "shard", split_axis=0, concat_axis=0, tiled=True)
    statistic = incoming.reshape(B, B)
    my_blocks = jnp.take(chosen, my_shard * OCAP + jnp.arange(OCAP, dtype=jnp.int32))
    mine_live = jnp.take(filled, my_shard * OCAP + slot_index)
    statistic = jnp.where(mine_live, statistic, jnp.eye(B, dtype=jnp.float32))
    factor = inverse_root(statistic)
    factors = lax.all_gather(factor[None], "dp", axis=0, tiled=True).reshape(OCAP, 2, B, B)
    grad_send = jnp.where(
        grad_live[:, :, None, None],
        pick(gradient, grad_pick),
        jnp.zeros((), jnp.bfloat16),
    )
    grad_full = lax.all_to_all(grad_send, "shard", split_axis=1, concat_axis=1, tiled=True).reshape(
        OCAP, B, B
    )
    result, grad_terms, result_terms = precondition(
        factors[:, 0], factors[:, 1], grad_full, member, quarter
    )
    layer_hot = (
        jnp.take(layer_of, my_blocks)[:, None] == jnp.arange(LAYERS, dtype=jnp.int32)[None, :]
    ).astype(jnp.float32)
    grad_total, result_total = lax.psum(
        (
            jnp.sum(layer_hot * grad_terms[:, None], axis=0),
            jnp.sum(layer_hot * result_terms[:, None], axis=0),
        ),
        ("dp", "shard"),
    )
    graft_ratio = jnp.sqrt((grad_total + 1e-06) / (result_total + 1e-06))
    scaled = (result * jnp.sum(layer_hot * graft_ratio[None, :], axis=1)[:, None, None]).astype(
        jnp.bfloat16
    )
    return scaled[None]


MESH = pl.DeviceIdType.MESH
PIECES = 2


def root_of(total):
    n = total.shape[0]

    def times(a, b):
        return jnp.dot(
            a.astype(jnp.bfloat16), b.astype(jnp.bfloat16), preferred_element_type=jnp.float32
        )

    mean_square = jnp.sum(total * total, axis=(0, 1), keepdims=True) * (1.0 / (n * n))
    magnitude = n * jnp.sqrt(mean_square + 1e-06)
    scale = 1.0 / jnp.sqrt(jnp.sqrt(magnitude))

    def next_matrix(quarter):
        w = 2.5 * quarter - times(quarter, quarter)
        v = 3.125 * w - times(w, w)
        return 2.44140625 * quarter - times(v, quarter)

    first = total * (0.25 / magnitude)
    second = next_matrix(first)
    both = 1.25 * (first + second) - times(first, second)
    third = next_matrix(second)
    rest = 1.25 * both + 1.5625 * third - times(both, third)
    rows = lax.broadcasted_iota(jnp.int32, (n, n), 0)
    columns = lax.broadcasted_iota(jnp.int32, (n, n), 1)
    return ((jnp.where(rows == columns, 1.953125, 0.0) - rest) * scale).astype(jnp.bfloat16)


def refresh(
    shards, stats_in, grad_in, owner_in, counts_in, out, theirs, ours, grad, owner, counts,
    xs, xr, ys, yr, keep, zs, whole, total, gcols, factor, mid, midr, raw, gath, vec, vecr, vecs, vecz,
    x_sem, y_sem, z_sem, g_sem, h_sem, m_sem, r_sem, a_sem, f_sem, n_sem, o_sem, l_sem,
):
    s = lax.axis_index("shard")
    m = lax.axis_index("dp")
    x, y = lax.rem(m, 2), m // 2
    blocks, rows, n = theirs.shape
    half, quarter = n // 2, n // 4
    piece = quarter // PIECES
    x_peer, y_peer = y * 2 + 1 - x, (1 - y) * 2 + x
    diagonal = (1 - y) * 2 + 1 - x

    loads = [
        pltpu.make_async_copy(source, target, l_sem.at[i])
        for i, (source, target) in enumerate(
            (
                (stats_in.at[:, 1 - x], theirs),
                (stats_in.at[:, x], ours),
                (grad_in, grad),
                (owner_in, owner),
                (counts_in, counts),
            )
        )
    ]
    for c in loads:
        c.start()
    barrier = pltpu.get_barrier_semaphore()
    for d in (x_peer, y_peer, diagonal):
        pl.semaphore_signal(barrier, inc=1, device_id=(d, s), device_id_type=MESH)
    for k in range(1, shards):
        pl.semaphore_signal(
            barrier, inc=1, device_id=(m, lax.rem(s + k, shards)), device_id_type=MESH
        )

    def remote(source, target, sems, i, device):
        return pltpu.make_async_remote_copy(
            src_ref=source, dst_ref=target, send_sem=sems.at[0, i], recv_sem=sems.at[1, i],
            device_id=device, device_id_type=MESH,
        )

    def columns(which):
        return pl.ds(pl.multiple_of(which * half, half), half)

    def own_rows(which):
        return pl.ds(pl.multiple_of(which * rows, rows), rows)

    order = [lax.rem(s + k, shards) for k in range(shards)]
    levels = shards // 2
    tile = n // levels
    pair, core = s // 2, lax.rem(s, 2)
    to = [
        2 * lax.rem(pair + k // 2, levels) + lax.rem(core + k % 2, 2) for k in range(blocks)
    ]
    tiles = [levels // 2 + (1 if k // 2 < levels // 2 else 0) for k in range(blocks)]

    def span(p):
        return pl.ds(pl.multiple_of(lax.rem(p, levels) * tile, tile), tile)

    def used(k):
        return pl.ds(0, tiles[k] * tile)

    def strip(ref, k):
        return jnp.concatenate([ref[to[k], :, span(pair + t)] for t in range(tiles[k])], axis=1)

    loads[0].wait()
    for k in range(blocks):
        xs[k, :, used(k)] = strip(theirs, k).astype(jnp.bfloat16)
    pl.semaphore_wait(barrier, shards + 2)

    x_copies, y_copies, z_copies, g_copies = [], [], [], []
    for k in range(blocks):
        c = remote(xs.at[k, :, used(k)], xr.at[k, :, used(k)], x_sem, k, (x_peer, s))
        c.start()
        x_copies.append(c)
    loads[1].wait()
    loads[2].wait()
    for k in range(1, shards):
        c = remote(
            grad.at[order[k], :, columns(y)], gcols.at[own_rows(s)], g_sem, k, (m, order[k])
        )
        c.start()
        g_copies.append(c)
    local = pltpu.make_async_copy(
        grad.at[s, :, columns(y)], gcols.at[own_rows(s)], l_sem.at[5]
    )
    local.start()
    lanes = lax.broadcasted_iota(jnp.int32, (8, 128), 1)
    lane_row = lax.broadcasted_iota(jnp.int32, (8, 128), 0)
    squares = jnp.zeros((8, 128), jnp.float32)
    for b in range(blocks):
        g = grad[b].astype(jnp.float32)
        squares = jnp.where(
            (lane_row == 1) & (lanes == b),
            jnp.sum(g * g, axis=(0, 1), keepdims=True) * 0.25,
            squares,
        )
    for t in range(blocks + 2):
        if t < blocks:
            x_copies[t].wait_recv()
            mine = strip(ours, t) + xr[t, :, used(t)].astype(jnp.float32)
            upper, lower = mine[: rows // 2], mine[rows // 2 :]
            keep[t, :, used(t)] = jnp.where(y == 0, upper, lower)
            ys[t, :, used(t)] = jnp.where(y == 0, lower, upper).astype(jnp.bfloat16)
            c = remote(ys.at[t, :, used(t)], yr.at[t, :, used(t)], y_sem, t, (y_peer, s))
            c.start()
            y_copies.append(c)
        if t >= 2:
            k = t - 2
            y_copies[k].wait_recv()
            both = (keep[k, :, used(k)] + yr[k, :, used(k)].astype(jnp.float32)).astype(
                jnp.bfloat16
            )
            if k == 0:
                whole[y, 0, :, used(0)] = both
            else:
                zs[k, :, used(k)] = both
                c = remote(
                    zs.at[k, :, used(k)], whole.at[y, k, :, used(k)], z_sem, k, (m, to[k])
                )
                c.start()
                z_copies.append(c)
    h_copies = []
    for k in range(blocks):
        if k > 0:
            z_copies[k - 1].wait_recv()
        at = whole.at[y, k, :, used(k)]
        c = remote(at, at, h_sem, k, (y_peer, s))
        c.start()
        h_copies.append(c)
    for d in range(levels):
        for e in range(2):
            h_copies[2 * d + e].wait_recv()
        source = lax.rem(pair + levels - d, levels)
        for t in range(tiles[2 * d]):
            at = pl.ds(t * tile, tile)
            block = jnp.concatenate(
                [
                    whole[u, 2 * d + lax.rem(core + c, 2), :, at].astype(jnp.float32)
                    for c in range(2)
                    for u in range(2)
                ],
                axis=0,
            )
            total[span(source), span(source + t)] = block
            if t > 0:
                total[span(source + t), span(source)] = block.T
    factor[...] = root_of(total[...])
    local.wait()
    for c in g_copies:
        c.wait_recv()

    neighbour = s + 1 - 2 * lax.rem(s, 2)

    def part(i):
        return pl.ds(i * piece, piece)

    def across(i):
        return remote(raw.at[part(i)], gath.at[s, part(i)], r_sem, i, (x_peer, s))

    def along(k, i):
        at = gath.at[s, part(i)]
        return remote(at, at, a_sem, k * PIECES + i, (m, order[2 * k]))

    def sideways(k, i):
        at = gath.at[lax.rem(s + shards - 2 * k, shards), part(i)]
        return remote(at, at, f_sem, k * PIECES + i, (m, neighbour))

    def spread(i):
        for k in range(1, levels):
            along(k, i).start()
        sideways(0, i).start()

    turns = [i + q * PIECES for q in (0, 1) for i in range(PIECES)]

    @pl.when(x == 0)
    def _():
        sent = []
        for t in turns:
            for slot, (side, d) in enumerate(((1 - y, diagonal), (y, x_peer))):
                at = pl.ds(pl.multiple_of(side * half + t * piece, piece), piece)
                mid[at] = jnp.dot(
                    factor[at], gcols[...], preferred_element_type=jnp.float32
                ).astype(jnp.bfloat16)
                c = remote(mid.at[at], midr.at[y, part(t)], m_sem, 2 * t + slot, (d, s))
                c.start()
                sent.append(c)
        vec[...] = squares
        for i in range(PIECES):
            across(i).wait_recv()
            spread(i)
        for c in sent:
            c.wait_send()

    @pl.when(x == 1)
    def _():
        squared = jnp.zeros((1, 1), jnp.float32)
        for t in turns:
            for slot, (source, d) in enumerate(((1 - y, diagonal), (y, x_peer))):
                at = midr.at[source, part(t)]
                remote(at, at, m_sem, 2 * t + slot, (d, s)).wait_recv()
            result = jnp.dot(
                midr[0, part(t)], factor[:half], preferred_element_type=jnp.float32
            ) + jnp.dot(midr[1, part(t)], factor[half:], preferred_element_type=jnp.float32)
            if t < PIECES:
                raw[part(t)] = result.astype(jnp.bfloat16)
                across(t).start()
            else:
                gath[s, part(t - PIECES)] = result.astype(jnp.bfloat16)
                spread(t - PIECES)
            squared = squared + jnp.sum(result * result, axis=(0, 1), keepdims=True)
        vec[...] = jnp.where((lane_row == 0) & (lanes == s), squared, squares)
        for i in range(PIECES):
            across(i).wait_send()

    norms = []
    for i, d in enumerate((x_peer, y_peer, diagonal)):
        c = remote(vec, vecr.at[i], n_sem, i, (d, s))
        c.start()
        norms.append(c)

    for c in norms:
        c.wait_recv()
    vecs[...] = vec[...] + vecr[0] + vecr[1] + vecr[2]
    for k in range(1, shards):
        c = remote(vecs, vecz.at[k - 1], o_sem, k, (m, order[k]))
        c.start()
        norms.append(c)
    for i in range(PIECES):
        for k in range(1, levels):
            along(k, i).wait_recv()
            sideways(k, i).start()
    for c in norms[3:]:
        c.wait_recv()
    loads[3].wait()
    loads[4].wait()
    totals = vecs[...] + jnp.sum(vecz[...], axis=0)
    raw_sq, grad_sq = totals[0:1], totals[1:2]

    ends, layer = [], []
    for l in range(counts.shape[0]):
        ends.append(counts[l] + (ends[-1] if ends else 0))
    for b in range(blocks):
        layer.append(sum(jnp.where(b >= e, 1, 0) for e in ends))
    count = jnp.int32(0)
    chosen = [jnp.int32(0)] * OCAP
    chosen_layer = [jnp.int32(-1)] * OCAP
    for b in range(blocks):
        is_mine = owner[b] == s
        for k in range(OCAP):
            hit = is_mine & (count == k)
            chosen[k] = jnp.where(hit, b, chosen[k])
            chosen_layer[k] = jnp.where(hit, layer[b], chosen_layer[k])
        count = count + jnp.where(is_mine, 1, 0)
    lane = lax.broadcasted_iota(jnp.int32, (1, 128), 1)
    layer_lane = jnp.full((1, 128), -2, jnp.int32)
    for b in range(blocks):
        layer_lane = jnp.where(lane == b, layer[b], layer_lane)
    scales = []
    for k in range(OCAP):
        same = layer_lane == chosen_layer[k]
        top = jnp.sum(jnp.where(same, grad_sq, 0.0), axis=1, keepdims=True)
        bottom = jnp.sum(jnp.where(same, raw_sq, 0.0), axis=1, keepdims=True)
        live = jnp.where(count > k, 1.0, 0.0)
        scales.append(live * jnp.sqrt((top + 1e-06) / (bottom + 1e-06)))

    for i in range(PIECES):
        for k in range(levels):
            sideways(k, i).wait_recv()
    for k in range(OCAP):
        out[k] = (gath[chosen[k]].astype(jnp.float32) * scales[k]).astype(jnp.bfloat16)
    for c in x_copies + y_copies + z_copies + g_copies + h_copies + norms:
        c.wait_send()
    for i in range(PIECES):
        for k in range(levels):
            sideways(k, i).wait_send()
            if k:
                along(k, i).wait_send()


def refreshed(stats_partial, gradient, owner_of, layer_count):
    shards = lax.axis_size("shard")
    stats = stats_partial[0]
    blocks, _, rows, n = stats.shape
    half, quarter = n // 2, n // 4
    width = n // 2 + n // (shards // 2)
    bf16, f32 = jnp.bfloat16, jnp.float32
    vmem = pltpu.VMEM
    sems = lambda count: pltpu.SemaphoreType.DMA((2, count))
    out = pl.pallas_call(
        functools.partial(refresh, shards),
        out_shape=jax.ShapeDtypeStruct((OCAP, quarter, n), bf16),
        in_specs=[pl.BlockSpec(memory_space=pltpu.HBM)] * 4,
        out_specs=pl.BlockSpec(memory_space=pltpu.VMEM),
        scratch_shapes=[
            vmem((blocks, rows, n), f32),
            vmem((blocks, rows, n), f32),
            vmem((blocks, rows, n), bf16),
            pltpu.SMEM(owner_of.shape, jnp.int32),
            pltpu.SMEM(layer_count.shape, jnp.int32),
            vmem((blocks, rows, width), bf16),
            vmem((blocks, rows, width), bf16),
            vmem((blocks, rows // 2, width), bf16),
            vmem((blocks, rows // 2, width), bf16),
            vmem((blocks, rows // 2, width), f32),
            vmem((blocks, rows // 2, width), bf16),
            vmem((2, blocks, rows // 2, width), bf16),
            vmem((n, n), f32),
            vmem((n, half), bf16),
            vmem((n, n), bf16),
            vmem((n, half), bf16),
            vmem((2, half, half), bf16),
            vmem((quarter, n), bf16),
            vmem((blocks, quarter, n), bf16),
            vmem((8, 128), f32),
            vmem((3, 8, 128), f32),
            vmem((8, 128), f32),
            vmem((shards - 1, 8, 128), f32),
            sems(blocks),
            sems(blocks),
            sems(blocks),
            sems(shards),
            sems(blocks),
            sems(4 * PIECES),
            sems(PIECES),
            sems(shards // 2 * PIECES),
            sems(shards // 2 * PIECES),
            sems(3),
            sems(shards),
            pltpu.SemaphoreType.DMA((7,)),
        ],
        compiler_params=pltpu.CompilerParams(
            collective_id=0, has_side_effects=True, vmem_limit_bytes=62 * 2**20
        ),
    )(stats, gradient, owner_of, layer_count)
    return out[None]


def solution(mesh):
    placed = (P("dp", None, None, "shard", None), P(None, "shard", None), P(), P())
    groups, shards = mesh.shape["dp"], mesh.shape["shard"]

    def program(stats_partial, gradient, owner_of, layer_count):
        blocks, strip = owner_of.shape[0], stats_partial.shape[3]
        fits = (groups, blocks) == (4, shards) and shards % 4 == 0 and strip % 64 == 0
        body = refreshed if fits and blocks <= 128 else on_device
        return body(stats_partial, gradient, owner_of, layer_count)

    return jax.shard_map(
        program,
        mesh=mesh,
        in_specs=placed,
        out_specs=P("shard", None, "dp", None),
        check_vma=False,
    )
```

```python
import functools

import jax
import jax.numpy as jnp
from jax import lax
from jax.experimental import pallas as pl
from jax.experimental.pallas import tpu as pltpu
from jax.sharding import PartitionSpec as P

B = 512
ITERS = 3
OCAP = 2
LAYERS = 4


highest = lax.Precision.HIGHEST


def product(left_side, right_side):
    return jnp.dot(left_side, right_side, precision=highest, preferred_element_type=jnp.float32)


def inverse_root(statistic):
    identity = jnp.eye(B, dtype=jnp.float32)
    magnitude = B * jnp.sqrt(jnp.mean(statistic * statistic) + 1e-06)
    matrix = statistic / magnitude
    factor = identity * magnitude ** (-0.25)
    for number in range(ITERS):
        update = (5.0 * identity - matrix) * 0.25
        factor = product(factor, update)
        if number + 1 < ITERS:
            square = product(update, update)
            fourth = product(square, square)
            matrix = product(fourth, matrix)
    return factor.astype(jnp.bfloat16)


def precondition(left_all, right_all, grad_full, member, quarter):
    left_rows = lax.dynamic_slice_in_dim(left_all, member * quarter, quarter, 1)
    middle = jnp.einsum(
        "kqb,kbc->kqc", left_rows, grad_full, preferred_element_type=jnp.float32
    ).astype(jnp.bfloat16)
    result = jnp.einsum("kqc,kcd->kqd", middle, right_all, preferred_element_type=jnp.float32)
    grad_rows = lax.dynamic_slice_in_dim(grad_full, member * quarter, quarter, 1).astype(
        jnp.float32
    )
    return (
        result,
        jnp.sum(grad_rows * grad_rows, axis=(1, 2)),
        jnp.sum(result * result, axis=(1, 2)),
    )


def pick(array, index):
    flat = lax.map(
        lambda i: lax.dynamic_index_in_dim(array, i, 0, keepdims=False), index.reshape(-1)
    )
    return flat.reshape(index.shape + array.shape[1:])


def on_device(stats_partial, gradient, owner_of, layer_count):
    shards = lax.axis_size("shard")
    groups = lax.axis_size("dp")
    my_shard = lax.axis_index("shard")
    member = lax.axis_index("dp")
    blocks = owner_of.shape[0]
    quarter = B // groups
    block_ids = jnp.arange(blocks, dtype=jnp.int32)
    same_owner = (owner_of[:, None] == owner_of[None, :]) & (
        block_ids[None, :] < block_ids[:, None]
    )
    earlier = jnp.sum(same_owner.astype(jnp.int32), axis=1)
    target = owner_of * OCAP + earlier
    places = jnp.arange(shards * OCAP, dtype=jnp.int32)
    matches = target[:, None] == places[None, :]
    filled = jnp.any(matches, axis=0)
    chosen = jnp.sum(jnp.where(matches, block_ids[:, None], 0), axis=0)
    all_places = (
        jnp.arange(OCAP, dtype=jnp.int32)[:, None]
        + OCAP * jnp.arange(shards, dtype=jnp.int32)[None, :]
    )
    grad_pick = jnp.take(chosen, all_places)
    grad_live = jnp.take(filled, all_places)
    layer_ids = jnp.arange(LAYERS)
    layer_ends = jnp.sum(
        jnp.where(layer_ids[:, None] <= layer_ids[None, :], layer_count[:, None], 0), axis=0
    )
    layer_of = jnp.sum((block_ids[:, None] >= layer_ends[None, :]).astype(jnp.int32), axis=1)
    local = stats_partial[0]
    local_rows = local.shape[2]
    slot_index = member // 2
    members = jnp.arange(groups, dtype=jnp.int32)
    place_all = jnp.arange(shards, dtype=jnp.int32)[None, :] * OCAP + (members // 2)[:, None]
    pick_all = jnp.take(chosen, place_all)
    live_all = jnp.take(filled, place_all)
    flat_local = local.reshape(blocks * 2, local_rows, B)
    laid = jnp.where(
        live_all[:, :, None, None],
        pick(flat_local, pick_all * 2 + (members % 2)[:, None]),
        0.0,
    )
    outgoing = lax.psum_scatter(laid, "dp", scatter_dimension=0, tiled=True)[0]
    incoming = lax.all_to_all(outgoing, "shard", split_axis=0, concat_axis=0, tiled=True)
    statistic = incoming.reshape(B, B)
    my_blocks = jnp.take(chosen, my_shard * OCAP + jnp.arange(OCAP, dtype=jnp.int32))
    mine_live = jnp.take(filled, my_shard * OCAP + slot_index)
    statistic = jnp.where(mine_live, statistic, jnp.eye(B, dtype=jnp.float32))
    factor = inverse_root(statistic)
    factors = lax.all_gather(factor[None], "dp", axis=0, tiled=True).reshape(OCAP, 2, B, B)
    grad_send = jnp.where(
        grad_live[:, :, None, None],
        pick(gradient, grad_pick),
        jnp.zeros((), jnp.bfloat16),
    )
    grad_full = lax.all_to_all(grad_send, "shard", split_axis=1, concat_axis=1, tiled=True).reshape(
        OCAP, B, B
    )
    result, grad_terms, result_terms = precondition(
        factors[:, 0], factors[:, 1], grad_full, member, quarter
    )
    layer_hot = (
        jnp.take(layer_of, my_blocks)[:, None] == jnp.arange(LAYERS, dtype=jnp.int32)[None, :]
    ).astype(jnp.float32)
    grad_total, result_total = lax.psum(
        (
            jnp.sum(layer_hot * grad_terms[:, None], axis=0),
            jnp.sum(layer_hot * result_terms[:, None], axis=0),
        ),
        ("dp", "shard"),
    )
    graft_ratio = jnp.sqrt((grad_total + 1e-06) / (result_total + 1e-06))
    scaled = (result * jnp.sum(layer_hot * graft_ratio[None, :], axis=1)[:, None, None]).astype(
        jnp.bfloat16
    )
    return scaled[None]


MESH = pl.DeviceIdType.MESH
PIECES = 2


def root_of(total):
    n = total.shape[0]

    def times(a, b):
        return jnp.dot(
            a.astype(jnp.bfloat16), b.astype(jnp.bfloat16), preferred_element_type=jnp.float32
        )

    mean_square = jnp.sum(total * total, axis=(0, 1), keepdims=True) * (1.0 / (n * n))
    magnitude = n * jnp.sqrt(mean_square + 1e-06)
    scale = 1.0 / jnp.sqrt(jnp.sqrt(magnitude))

    def next_matrix(quarter):
        w = 2.5 * quarter - times(quarter, quarter)
        v = 3.125 * w - times(w, w)
        return 2.44140625 * quarter - times(v, quarter)

    first = total * (0.25 / magnitude)
    second = next_matrix(first)
    both = 1.25 * (first + second) - times(first, second)
    third = next_matrix(second)
    rest = 1.25 * both + 1.5625 * third - times(both, third)
    rows = lax.broadcasted_iota(jnp.int32, (n, n), 0)
    columns = lax.broadcasted_iota(jnp.int32, (n, n), 1)
    return ((jnp.where(rows == columns, 1.953125, 0.0) - rest) * scale).astype(jnp.bfloat16)


def refresh(
    shards, stats_in, grad_in, owner_in, counts_in, out, theirs, ours, grad, owner, counts,
    xs, xr, ys, yr, keep, zs, whole, total, gcols, factor, mid, midr, raw, gath, vec, vecr, vecs, vecz,
    x_sem, y_sem, z_sem, g_sem, h_sem, m_sem, r_sem, a_sem, p_sem, f_sem, n_sem, o_sem, l_sem,
):
    s = lax.axis_index("shard")
    m = lax.axis_index("dp")
    x, y = lax.rem(m, 2), m // 2
    blocks, rows, n = theirs.shape
    half, quarter = n // 2, n // 4
    piece = quarter // PIECES
    x_peer, y_peer = y * 2 + 1 - x, (1 - y) * 2 + x
    diagonal = (1 - y) * 2 + 1 - x

    loads = [
        pltpu.make_async_copy(source, target, l_sem.at[i])
        for i, (source, target) in enumerate(
            (
                (stats_in.at[:, 1 - x], theirs),
                (stats_in.at[:, x], ours),
                (grad_in, grad),
                (owner_in, owner),
                (counts_in, counts),
            )
        )
    ]
    for c in loads:
        c.start()
    barrier = pltpu.get_barrier_semaphore()
    for d in (x_peer, y_peer, diagonal):
        pl.semaphore_signal(barrier, inc=1, device_id=(d, s), device_id_type=MESH)
    for k in range(1, shards):
        pl.semaphore_signal(
            barrier, inc=1, device_id=(m, lax.rem(s + k, shards)), device_id_type=MESH
        )

    def remote(source, target, sems, i, device):
        return pltpu.make_async_remote_copy(
            src_ref=source, dst_ref=target, send_sem=sems.at[0, i], recv_sem=sems.at[1, i],
            device_id=device, device_id_type=MESH,
        )

    def columns(which):
        return pl.ds(pl.multiple_of(which * half, half), half)

    def own_rows(which):
        return pl.ds(pl.multiple_of(which * rows, rows), rows)

    order = [lax.rem(s + k, shards) for k in range(shards)]
    levels = shards // 2
    tile = n // levels
    pair, core = s // 2, lax.rem(s, 2)
    to = [
        2 * lax.rem(pair + k // 2, levels) + lax.rem(core + k % 2, 2) for k in range(blocks)
    ]
    tiles = [levels // 2 + (1 if k // 2 < levels // 2 else 0) for k in range(blocks)]

    def span(p):
        return pl.ds(pl.multiple_of(lax.rem(p, levels) * tile, tile), tile)

    def used(k):
        return pl.ds(0, tiles[k] * tile)

    def strip(ref, k):
        return jnp.concatenate([ref[to[k], :, span(pair + t)] for t in range(tiles[k])], axis=1)

    loads[0].wait()
    for k in range(blocks):
        xs[k, :, used(k)] = strip(theirs, k).astype(jnp.bfloat16)
    pl.semaphore_wait(barrier, shards + 2)

    x_copies, y_copies, z_copies, g_copies = [], [], [], []
    for k in range(blocks):
        c = remote(xs.at[k, :, used(k)], xr.at[k, :, used(k)], x_sem, k, (x_peer, s))
        c.start()
        x_copies.append(c)
    loads[1].wait()
    loads[2].wait()
    for k in range(1, shards):
        c = remote(
            grad.at[order[k], :, columns(y)], gcols.at[own_rows(s)], g_sem, k, (m, order[k])
        )
        c.start()
        g_copies.append(c)
    local = pltpu.make_async_copy(
        grad.at[s, :, columns(y)], gcols.at[own_rows(s)], l_sem.at[5]
    )
    local.start()
    lanes = lax.broadcasted_iota(jnp.int32, (8, 128), 1)
    lane_row = lax.broadcasted_iota(jnp.int32, (8, 128), 0)
    squares = jnp.zeros((8, 128), jnp.float32)
    for b in range(blocks):
        g = grad[b].astype(jnp.float32)
        squares = jnp.where(
            (lane_row == 1) & (lanes == b),
            jnp.sum(g * g, axis=(0, 1), keepdims=True) * 0.25,
            squares,
        )
    for t in range(blocks + 2):
        if t < blocks:
            x_copies[t].wait_recv()
            mine = strip(ours, t) + xr[t, :, used(t)].astype(jnp.float32)
            upper, lower = mine[: rows // 2], mine[rows // 2 :]
            keep[t, :, used(t)] = jnp.where(y == 0, upper, lower)
            ys[t, :, used(t)] = jnp.where(y == 0, lower, upper).astype(jnp.bfloat16)
            c = remote(ys.at[t, :, used(t)], yr.at[t, :, used(t)], y_sem, t, (y_peer, s))
            c.start()
            y_copies.append(c)
        if t >= 2:
            k = t - 2
            y_copies[k].wait_recv()
            both = (keep[k, :, used(k)] + yr[k, :, used(k)].astype(jnp.float32)).astype(
                jnp.bfloat16
            )
            if k == 0:
                whole[y, 0, :, used(0)] = both
            else:
                zs[k, :, used(k)] = both
                c = remote(
                    zs.at[k, :, used(k)], whole.at[y, k, :, used(k)], z_sem, k, (m, to[k])
                )
                c.start()
                z_copies.append(c)
    h_copies = []
    for k in range(blocks):
        if k > 0:
            z_copies[k - 1].wait_recv()
        at = whole.at[y, k, :, used(k)]
        c = remote(at, at, h_sem, k, (y_peer, s))
        c.start()
        h_copies.append(c)
    for d in range(levels):
        for e in range(2):
            h_copies[2 * d + e].wait_recv()
        source = lax.rem(pair + levels - d, levels)
        for t in range(tiles[2 * d]):
            at = pl.ds(t * tile, tile)
            block = jnp.concatenate(
                [
                    whole[u, 2 * d + lax.rem(core + c, 2), :, at].astype(jnp.float32)
                    for c in range(2)
                    for u in range(2)
                ],
                axis=0,
            )
            total[span(source), span(source + t)] = block
            if t > 0:
                total[span(source + t), span(source)] = block.T
    factor[...] = root_of(total[...])
    local.wait()
    for c in g_copies:
        c.wait_recv()

    neighbour = s + 1 - 2 * lax.rem(s, 2)

    def part(i):
        return pl.ds(i * piece, piece)

    def across(i):
        return remote(raw.at[part(i)], gath.at[s, part(i)], r_sem, i, (x_peer, s))

    def along(k, i):
        at = gath.at[s, part(i)]
        return remote(at, at, a_sem, k * PIECES + i, (m, order[2 * k]))

    def sideways(k, i):
        at = gath.at[lax.rem(s + shards - 2 * k, shards), part(i)]
        return remote(at, at, f_sem, k * PIECES + i, (m, neighbour))

    def spread(i):
        for k in turned:
            if k in (1, levels - 1):

                @pl.when(pair != (levels - 1 if k == 1 else 0))
                def _():
                    along(k, i).start()

            else:
                along(k, i).start()
        sideways(0, i).start()

    turned = [2] + [k for k in range(1, levels) if k != 2]

    def passed(up, i):
        back, k = (levels - 2, levels - 1) if up else (2, 1)
        at = gath.at[lax.rem(s + shards - 2 * back, shards), part(i)]
        return pltpu.make_async_remote_copy(
            src_ref=at, dst_ref=at, send_sem=p_sem.at[int(up), i],
            recv_sem=a_sem.at[1, k * PIECES + i],
            device_id=(m, order[2 if up else shards - 2]), device_id_type=MESH,
        )

    turns = [i + q * PIECES for q in (0, 1) for i in range(PIECES)]

    @pl.when(x == 0)
    def _():
        sent = []
        for t in turns:
            for slot, (side, d) in enumerate(((1 - y, diagonal), (y, x_peer))):
                at = pl.ds(pl.multiple_of(side * half + t * piece, piece), piece)
                mid[at] = jnp.dot(
                    factor[at], gcols[...], preferred_element_type=jnp.float32
                ).astype(jnp.bfloat16)
                c = remote(mid.at[at], midr.at[y, part(t)], m_sem, 2 * t + slot, (d, s))
                c.start()
                sent.append(c)
        vec[...] = squares
        for i in range(PIECES):
            across(i).wait_recv()
            spread(i)
        for c in sent:
            c.wait_send()

    @pl.when(x == 1)
    def _():
        squared = jnp.zeros((1, 1), jnp.float32)
        for t in turns:
            for slot, (source, d) in enumerate(((1 - y, diagonal), (y, x_peer))):
                at = midr.at[source, part(t)]
                remote(at, at, m_sem, 2 * t + slot, (d, s)).wait_recv()
            result = jnp.dot(
                midr[0, part(t)], factor[:half], preferred_element_type=jnp.float32
            ) + jnp.dot(midr[1, part(t)], factor[half:], preferred_element_type=jnp.float32)
            if t < PIECES:
                raw[part(t)] = result.astype(jnp.bfloat16)
                across(t).start()
            else:
                gath[s, part(t - PIECES)] = result.astype(jnp.bfloat16)
                spread(t - PIECES)
            squared = squared + jnp.sum(result * result, axis=(0, 1), keepdims=True)
        vec[...] = jnp.where((lane_row == 0) & (lanes == s), squared, squares)
        for i in range(PIECES):
            across(i).wait_send()

    norms = []
    for i, d in enumerate((x_peer, y_peer, diagonal)):
        c = remote(vec, vecr.at[i], n_sem, i, (d, s))
        c.start()
        norms.append(c)

    for c in norms:
        c.wait_recv()
    vecs[...] = vec[...] + vecr[0] + vecr[1] + vecr[2]
    for k in range(1, shards):
        c = remote(vecs, vecz.at[k - 1], o_sem, k, (m, order[k]))
        c.start()
        norms.append(c)
    first = sorted({2, levels - 2})
    for ks in (first, [k for k in range(1, levels) if k not in first]):
        for i in range(PIECES):
            for k in ks:
                along(k, i).wait_recv()
                if k == levels - 2:

                    @pl.when(pair == levels - 2)
                    def _():
                        passed(True, i).start()

                if k == 2:

                    @pl.when(pair == 1)
                    def _():
                        passed(False, i).start()

                sideways(k, i).start()
    for c in norms[3:]:
        c.wait_recv()
    loads[3].wait()
    loads[4].wait()
    totals = vecs[...] + jnp.sum(vecz[...], axis=0)
    raw_sq, grad_sq = totals[0:1], totals[1:2]

    ends, layer = [], []
    for l in range(counts.shape[0]):
        ends.append(counts[l] + (ends[-1] if ends else 0))
    for b in range(blocks):
        layer.append(sum(jnp.where(b >= e, 1, 0) for e in ends))
    count = jnp.int32(0)
    chosen = [jnp.int32(0)] * OCAP
    chosen_layer = [jnp.int32(-1)] * OCAP
    for b in range(blocks):
        is_mine = owner[b] == s
        for k in range(OCAP):
            hit = is_mine & (count == k)
            chosen[k] = jnp.where(hit, b, chosen[k])
            chosen_layer[k] = jnp.where(hit, layer[b], chosen_layer[k])
        count = count + jnp.where(is_mine, 1, 0)
    lane = lax.broadcasted_iota(jnp.int32, (1, 128), 1)
    layer_lane = jnp.full((1, 128), -2, jnp.int32)
    for b in range(blocks):
        layer_lane = jnp.where(lane == b, layer[b], layer_lane)
    scales = []
    for k in range(OCAP):
        same = layer_lane == chosen_layer[k]
        top = jnp.sum(jnp.where(same, grad_sq, 0.0), axis=1, keepdims=True)
        bottom = jnp.sum(jnp.where(same, raw_sq, 0.0), axis=1, keepdims=True)
        live = jnp.where(count > k, 1.0, 0.0)
        scales.append(live * jnp.sqrt((top + 1e-06) / (bottom + 1e-06)))

    for i in range(PIECES):
        for k in range(levels):
            sideways(k, i).wait_recv()
    for k in range(OCAP):
        out[k] = (gath[chosen[k]].astype(jnp.float32) * scales[k]).astype(jnp.bfloat16)
    for c in x_copies + y_copies + z_copies + g_copies + h_copies + norms:
        c.wait_send()
    for i in range(PIECES):
        for k in range(levels):
            sideways(k, i).wait_send()
            if k in (1, levels - 1):

                @pl.when(pair != (levels - 1 if k == 1 else 0))
                def _():
                    along(k, i).wait_send()

            elif k:
                along(k, i).wait_send()

        @pl.when(pair == levels - 2)
        def _():
            passed(True, i).wait_send()

        @pl.when(pair == 1)
        def _():
            passed(False, i).wait_send()


def refreshed(stats_partial, gradient, owner_of, layer_count):
    shards = lax.axis_size("shard")
    stats = stats_partial[0]
    blocks, _, rows, n = stats.shape
    half, quarter = n // 2, n // 4
    width = n // 2 + n // (shards // 2)
    bf16, f32 = jnp.bfloat16, jnp.float32
    vmem = pltpu.VMEM
    sems = lambda count: pltpu.SemaphoreType.DMA((2, count))
    out = pl.pallas_call(
        functools.partial(refresh, shards),
        out_shape=jax.ShapeDtypeStruct((OCAP, quarter, n), bf16),
        in_specs=[pl.BlockSpec(memory_space=pltpu.HBM)] * 4,
        out_specs=pl.BlockSpec(memory_space=pltpu.VMEM),
        scratch_shapes=[
            vmem((blocks, rows, n), f32),
            vmem((blocks, rows, n), f32),
            vmem((blocks, rows, n), bf16),
            pltpu.SMEM(owner_of.shape, jnp.int32),
            pltpu.SMEM(layer_count.shape, jnp.int32),
            vmem((blocks, rows, width), bf16),
            vmem((blocks, rows, width), bf16),
            vmem((blocks, rows // 2, width), bf16),
            vmem((blocks, rows // 2, width), bf16),
            vmem((blocks, rows // 2, width), f32),
            vmem((blocks, rows // 2, width), bf16),
            vmem((2, blocks, rows // 2, width), bf16),
            vmem((n, n), f32),
            vmem((n, half), bf16),
            vmem((n, n), bf16),
            vmem((n, half), bf16),
            vmem((2, half, half), bf16),
            vmem((quarter, n), bf16),
            vmem((blocks, quarter, n), bf16),
            vmem((8, 128), f32),
            vmem((3, 8, 128), f32),
            vmem((8, 128), f32),
            vmem((shards - 1, 8, 128), f32),
            sems(blocks),
            sems(blocks),
            sems(blocks),
            sems(shards),
            sems(blocks),
            sems(4 * PIECES),
            sems(PIECES),
            sems(shards // 2 * PIECES),
            sems(PIECES),
            sems(shards // 2 * PIECES),
            sems(3),
            sems(shards),
            pltpu.SemaphoreType.DMA((7,)),
        ],
        compiler_params=pltpu.CompilerParams(
            collective_id=0, has_side_effects=True, vmem_limit_bytes=62 * 2**20
        ),
    )(stats, gradient, owner_of, layer_count)
    return out[None]


def solution(mesh):
    placed = (P("dp", None, None, "shard", None), P(None, "shard", None), P(), P())
    groups, shards = mesh.shape["dp"], mesh.shape["shard"]

    def program(stats_partial, gradient, owner_of, layer_count):
        blocks, strip = owner_of.shape[0], stats_partial.shape[3]
        fits = (groups, blocks) == (4, shards) and shards % 4 == 0 and shards >= 8
        fits = fits and strip % 64 == 0
        body = refreshed if fits and blocks <= 128 else on_device
        return body(stats_partial, gradient, owner_of, layer_count)

    return jax.shard_map(
        program,
        mesh=mesh,
        in_specs=placed,
        out_specs=P("shard", None, "dp", None),
        check_vma=False,
    )
```
